512 devices in a mesh: dp: 32 (over z, y_hi), tensor: 16 (over x, y_lo, core).
Axes of the slice: x: 4, y: 8 (y_hi: 4, y_lo: 2; y = y_hi * 2 + y_lo), z: 8, core: 2. Of those that a mesh axis runs over, the one named last changes fastest.
Arguments:
- tokens: bfloat16 [512, 8192], P('dp', 'tensor'), may hold values from -6 to 6
- out_grad: bfloat16 [512, 8192], P('dp', 'tensor'), may hold values from -6 to 6
- gate_weight: bfloat16 [8192, 14336], P('tensor', 'dp'), may hold values from -0.0625 to 0.0625
- up_weight: bfloat16 [8192, 14336], P('tensor', 'dp'), may hold values from -0.0625 to 0.0625
- down_weight: bfloat16 [14336, 8192], P('dp', 'tensor'), may hold values from -0.0625 to 0.0625
- pair_list: int32 [512, 2], P(('dp', 'tensor')), may hold values from 0 to 31, as said below
Outputs:
- act_cov: float32 [512, 448, 448], P(('dp', 'tensor'))
- grad_cov: float32 [512, 448, 448], P(('dp', 'tensor'))
The draws below stay inside these ranges and needn't reach their ends.
Inputs may be any that keep to these rules, and one draw needn't show every extreme that they name: `pair_list`: row 16 * i + j is (i, (i + e_j) mod 32), where e is one permutation of 1 to 16 shared by every i.
All inputs are finite; a program needn't handle non-finite values.
Results may differ from the reference program's by a relative error of at most 0.004.
Values may be sent and summed in bfloat16 or wider, within the bound.
A program may use at most 64 MiB of HBM per device.

```python
import jax
import jax.numpy as jnp
from jax import lax

D = 8192
FF = 14336
TOKENS = 512
NBLK = 32
BLOCK = 448
HALF = 16
DSLICE = 512


def draw_pair_list(key, part):
    key = jax.random.fold_in(key, 7)
    distances = jax.random.permutation(key, HALF).astype(jnp.int32) + 1
    own_block = jnp.arange(NBLK, dtype=jnp.int32)[:, None] * jnp.ones((1, HALF), jnp.int32)
    far_block = (own_block + distances[None, :]) % NBLK
    return jnp.stack([own_block.reshape(-1), far_block.reshape(-1)], axis=1).astype(jnp.int32)


def steps_of(key, extent, cuts, low, largest):
    factor_of = 1.0
    for axis_at, parts in cuts:
        draws = jax.random.uniform(jax.random.fold_in(jax.random.fold_in(key, 6), axis_at), (parts,), jnp.float32, low / len(cuts), largest / len(cuts))
        factor_of = factor_of * jnp.repeat(jnp.exp(draws), extent[axis_at] // parts).reshape((-1,) + (1,) * (len(extent) - 1 - axis_at))
    return factor_of


def centred(stream_key, extent, deviation, bound, split=(), kind=jnp.bfloat16):
    drawn = jax.random.normal(stream_key, extent, jnp.float32) * deviation
    if len(split) > 0:
        drawn = steps_of(stream_key, extent, split, -0.22, 0.18) * drawn
    return jnp.clip(drawn, min=-bound, max=bound).astype(kind)


def setup_inputs(seed: int = 0) -> dict:
    streams_of = jax.random.split(jax.random.key(seed), 7)
    return {
        "tokens": centred(streams_of[0], (TOKENS, D), 1.0, 6.0, ((0, 32), (1, 16))),
        "out_grad": centred(streams_of[1], (TOKENS, D), 1.0, 6.0, ((0, 32), (1, 16))),
        "gate_weight": centred(streams_of[2], (D, FF), D ** -0.5, 0.0625, ((0, 16), (1, 32))),
        "up_weight": centred(streams_of[3], (D, FF), D ** -0.5, 0.0625, ((0, 16), (1, 32))),
        "down_weight": centred(streams_of[4], (FF, D), D ** -0.5, 0.0625, ((0, 32), (1, 16))),
        "pair_list": draw_pair_list(jax.random.fold_in(streams_of[6], 71), 0),
    }


def reference(tokens, out_grad, gate_weight, up_weight, down_weight, pair_list):
    token_parts = tokens.reshape(TOKENS, HALF, DSLICE).transpose(1, 0, 2)
    grad_parts = out_grad.reshape(TOKENS, HALF, DSLICE).transpose(1, 0, 2)
    gate_parts = gate_weight.reshape(HALF, DSLICE, FF)
    up_parts = up_weight.reshape(HALF, DSLICE, FF)
    down_parts = down_weight.reshape(FF, HALF, DSLICE).transpose(1, 0, 2)

    def accumulate(running, pieces):
        token_part, grad_part, gate_part, up_part, down_part = pieces
        gate_sum = running[0] + jnp.dot(token_part, gate_part, preferred_element_type=jnp.float32)
        up_sum = running[1] + jnp.dot(token_part, up_part, preferred_element_type=jnp.float32)
        grad_sum = running[2] + jnp.dot(grad_part, down_part.T, preferred_element_type=jnp.float32)
        return (gate_sum, up_sum, grad_sum), None

    empty_sum = jnp.zeros((TOKENS, FF), jnp.float32)
    (gate_sum, up_sum, grad_sum), _ = lax.scan(accumulate, (empty_sum, empty_sum, empty_sum),
                                               (token_parts, grad_parts, gate_parts, up_parts, down_parts))
    hidden = (jax.nn.silu(gate_sum) * up_sum).astype(jnp.bfloat16)
    hidden_grad = grad_sum.astype(jnp.bfloat16)
    inverse = 1.0 / TOKENS
    row_ids = lax.broadcasted_iota(jnp.int32, (BLOCK, BLOCK), 0)
    col_ids = lax.broadcasted_iota(jnp.int32, (BLOCK, BLOCK), 1)
    upper_mask = row_ids <= col_ids

    def tile_of(matrix, own_index, far_index, diagonal):
        own_block = lax.dynamic_slice_in_dim(matrix, own_index * BLOCK, BLOCK, 1)
        far_block = lax.dynamic_slice_in_dim(matrix, far_index * BLOCK, BLOCK, 1)

        def cross_tile(own_block, far_block):
            return jnp.dot(own_block.T, far_block, preferred_element_type=jnp.float32)

        def diagonal_tile(own_block, far_block):
            own_gram = jnp.dot(own_block.T, own_block, preferred_element_type=jnp.float32)
            far_gram = jnp.dot(far_block.T, far_block, preferred_element_type=jnp.float32)
            return jnp.where(upper_mask, own_gram, far_gram)

        return lax.cond(diagonal, diagonal_tile, cross_tile, own_block, far_block) * inverse

    def one_item(pair_row):
        own_index = pair_row[0].astype(jnp.int32)
        far_index = pair_row[1].astype(jnp.int32)
        diagonal = ((far_index - own_index) % NBLK == HALF) & (own_index >= HALF)
        return (tile_of(hidden, own_index, far_index, diagonal),
                tile_of(hidden_grad, own_index, far_index, diagonal))

    act_cov, grad_cov = lax.map(one_item, pair_list)
    return act_cov, grad_cov
```

```python
import jax
import jax.numpy as jnp
from jax import lax
from jax.experimental import pallas as pl
from jax.experimental.pallas import tpu as pltpu
from jax.sharding import PartitionSpec as P

Z, YH, X, YL, CORES = 8, 4, 4, 2, 2
DP, GROUP = Z * YH, X * YL * CORES
CHIPS = X * YL
LEVELS = 32760.0
MESH = pl.DeviceIdType.MESH
f32, bf16, i16, i32 = jnp.float32, jnp.bfloat16, jnp.int16, jnp.int32


def encode(value, largest):
    root = jnp.sqrt(jnp.abs(value)) * (LEVELS * lax.rsqrt(largest))
    code = (root + 0.5).astype(i32)
    return jnp.where(value < 0, -code, code).astype(i16)


def decode(code, unit):
    root = code.astype(i32).astype(f32)
    return root * jnp.abs(root) * unit


def fold(rows):
    half = rows.shape[0] // 2
    return jnp.concatenate([rows[:half], rows[half:]], axis=1)


def unfold(folded):
    width = folded.shape[1] // 2
    return jnp.concatenate([folded[:, :width], folded[:, width:]], axis=0)


def kernel(tok_in, grd_in, wg_in, wu_in, wd_in, pair, act_out, grad_out,
           x_tok, x_grd, wg, wu, wd, pair_tiles, pair_smem,
           ps_act, pr_act, ps_grd, pr_grd, sum_act, sum_grd,
           cs_act, cr_act, cs_grd, cr_grd, us_act, ur_act, us_grd, ur_grd,
           own_act, own_grd, far_act, far_grd, st_act, st_grd, b_act, b_grd,
           tile_act, tile_grd, local_sem, send_sem, recv_sem):
    dp, tensor = lax.axis_index("dp"), lax.axis_index("tensor")
    z, yh = dp // YH, dp % YH
    core, chip = tensor % CORES, tensor // CORES
    x, yl = chip // YL, chip % YL

    def at(dz=0, dyh=0):
        return ((z + dz + Z) % Z * YH + (yh + dyh + YH) % YH, tensor)

    def in_group(dx, dyl, dc, sign=1):
        return (((x + sign * dx + X) % X * YL + (yl + dyl) % YL) * CORES + (core + dc) % CORES)

    used = [0]
    started = []

    def remote(src, dst, device):
        n = used[0]
        used[0] += 1
        return pltpu.make_async_remote_copy(
            src_ref=src, dst_ref=dst, send_sem=send_sem.at[n], recv_sem=recv_sem.at[n],
            device_id=device, device_id_type=MESH)

    def send(src, dst, device):
        copy = remote(src, dst, device)
        copy.start()
        started.append(copy)
        return copy

    peers = [(dx, dyl, dc) for dx in (2, 1, 3, 0) for dyl in (1, 0) for dc in (0, 1) if (dx, dyl, dc) != (0, 0, 0)]
    chip_peers = [(dx, dyl) for dx in (2, 1, 3, 0) for dyl in (1, 0) if (dx, dyl) != (0, 0)]

    loads = [pltpu.make_async_copy(tok_in, x_tok.at[dp], local_sem.at[0]),
             pltpu.make_async_copy(grd_in, x_grd.at[dp], local_sem.at[1]),
             pltpu.make_async_copy(wg_in, wg, local_sem.at[2]),
             pltpu.make_async_copy(wu_in, wu, local_sem.at[3]),
             pltpu.make_async_copy(wd_in, wd, local_sem.at[4])]
    for load in loads:
        load.start()
    barrier = pltpu.get_barrier_semaphore()
    partners = [at(dyh=k) for k in (1, 2, 3)] + [at(dz=1), at(dz=-1)] + [(dp, in_group(*o)) for o in peers]
    for partner in partners:
        pl.semaphore_signal(barrier, inc=1, device_id=partner, device_id_type=MESH)
    distance = (pair[0, 1] - pair[0, 0] + DP) % DP
    pair_tiles[tensor] = jnp.full((8, 128), distance, i32)
    pl.semaphore_wait(barrier, len(partners))

    loads[0].wait()
    loads[1].wait()
    bufs = (x_tok, x_grd)
    from_y = [[None] * YH for _ in bufs]
    ring = {}
    for b, buf in enumerate(bufs):
        for k in (2, 1, 3):
            from_y[b][k] = send(buf.at[dp], buf.at[dp], at(dyh=k))
        for way in (1, -1):
            ring[b, way, 0, 0] = send(buf.at[dp], buf.at[dp], at(dz=way))
    pair_copies = [send(pair_tiles.at[tensor], pair_tiles.at[tensor], (dp, in_group(*o))) for o in peers]
    for k in (1, 3, 2):
        for b, buf in enumerate(bufs):
            from_y[b][k].wait_recv()
            slot = z * YH + (yh - k + YH) % YH
            for way in (1, -1):
                ring[b, way, 0, k] = send(buf.at[slot], buf.at[slot], at(dz=way))
    for hop in (1, 2, 3):
        for b, buf in enumerate(bufs):
            for way in (1, -1):
                for k in range(YH if hop == 1 else 1):
                    ring[b, way, hop - 1, k].wait_recv()
                source = (z - way * hop + Z) % Z * YH
                if hop < 3:
                    rows = pl.ds(source, YH)
                else:
                    rows = pl.ds(source + (0 if way == 1 else YH // 2), YH // 2)
                ring[b, way, hop, 0] = send(buf.at[rows], buf.at[rows], at(dz=way))
    for load in loads[2:]:
        load.wait()

    def rows_of(buf, half):
        return buf[pl.ds(half * (DP // 2), DP // 2)].reshape(buf.shape[1] * DP // 2, buf.shape[2])

    def act_products(half):
        rows = rows_of(x_tok, half)
        return (fold(jnp.dot(rows, wg[...], preferred_element_type=f32)),
                fold(jnp.dot(rows, wu[...], preferred_element_type=f32)))

    def grd_products(half):
        return (fold(lax.dot_general(rows_of(x_grd, half), wd[...], (((1,), (1,)), ((), ())),
                                     preferred_element_type=f32)),)

    other = (dp, in_group(0, 0, 1))
    piece = 16

    def reduce_pair(b, products, ps, pr, total, cs, us):
        for way in (1, -1):
            ring[b, way, 3, 0].wait_recv()
        for i, product in enumerate(products(1 - core)):
            ps[i] = product
        pair = send(ps, pr, other)
        for i, product in enumerate(products(core)):
            total[i] = product
        pair.wait_recv()
        largest = []
        for i in range(total.shape[0]):
            summed = total[i] + pr[i]
            total[i] = summed
            largest.append(jnp.maximum(jnp.max(jnp.abs(summed)), 1e-30))
        for i, most in enumerate(largest):
            us[i] = jnp.full((8, 128), most * (1.0 / (LEVELS * LEVELS)), f32)
            cs[:, i] = encode(total[i], most).reshape(CHIPS, piece, total.shape[2])

    def spread(cs, cr, us, ur):
        copies = []
        for n, (dx, dyl) in enumerate(chip_peers):
            there = in_group(dx, dyl, 0)
            copies.append((send(us, ur.at[n], (dp, there)),
                           send(cs.at[there // CORES], cr.at[n], (dp, there))))
        return copies

    def gathered(copies, total, cr, ur):
        mine = [total[i, pl.ds(chip * piece, piece)] for i in range(total.shape[0])]
        for n, copy in enumerate(copies):
            for c in copy:
                c.wait_recv()
            for i in range(total.shape[0]):
                mine[i] += decode(cr[n, i], ur[n, i, 0:1, 0:1])
        return mine

    reduce_pair(0, act_products, ps_act, pr_act, sum_act, cs_act, us_act)
    c_act = spread(cs_act, cr_act, us_act, ur_act)
    reduce_pair(1, grd_products, ps_grd, pr_grd, sum_grd, cs_grd, us_grd)
    c_grd = spread(cs_grd, cr_grd, us_grd, ur_grd)

    def share_out(own):
        first = [send(own.at[tensor], own.at[tensor], (dp, in_group(dx, dyl, 0))) for dx, dyl in chip_peers]
        return first, [send(own.at[tensor], own.at[tensor], other)]

    def pass_on(own, first, second):
        for (dx, dyl), copy in zip(chip_peers, first):
            copy.wait_recv()
            slot = in_group(dx, dyl, 0, sign=-1)
            second.append(send(own.at[slot], own.at[slot], other))

    gate, up = gathered(c_act, sum_act, cr_act, ur_act)
    hidden = (gate / (1.0 + jnp.exp(-gate)) * up).astype(bf16)
    own_act[tensor] = hidden
    far_act[yh] = hidden
    act_y = {k: send(far_act.at[yh], far_act.at[yh], at(dyh=k)) for k in (2, 1, 3)}
    act_z = {(0, 0): send(far_act.at[yh], far_act.at[YH + yh], at(dz=-1))}
    d_act = share_out(own_act)

    (grad_sum,) = gathered(c_grd, sum_grd, cr_grd, ur_grd)
    hidden_grad = grad_sum.astype(bf16)
    own_grd[tensor] = hidden_grad
    far_grd[yh] = hidden_grad
    grd_z = [send(far_grd.at[yh], far_grd.at[YH + yh], at(dz=-1))]
    d_grd = share_out(own_grd)

    for k in (1, 3, 2):
        act_y[k].wait_recv()
        slot = (yh - k + YH) % YH
        act_z[0, k] = send(far_act.at[slot], far_act.at[YH + slot], at(dz=-1))

    grd_y = {}
    for k in (2, 1, 3):
        grd_y[0, k] = remote(far_grd.at[yh], far_grd.at[yh], at(dyh=k))
        pl.when((yh + k) % YH < yh)(grd_y[0, k].start)
    for hop in (1, 2, 3, 4):
        slot = hop * YH + yh
        grd_z[hop - 1].wait_recv()
        if hop < 4:
            grd_z.append(send(far_grd.at[slot], far_grd.at[slot + YH], at(dz=-1)))
        for k in (2, 1, 3):
            grd_y[hop, k] = remote(far_grd.at[slot], far_grd.at[slot], at(dyh=k))
            if hop < 4:
                grd_y[hop, k].start()
                started.append(grd_y[hop, k])
            else:
                pl.when((yh + k) % YH > yh)(grd_y[hop, k].start)
        if hop < 4:
            for k in range(YH):
                there = (yh - k + YH) % YH
                act_z[hop - 1, k].wait_recv()
                row = hop * YH + there
                act_z[hop, k] = remote(far_act.at[row], far_act.at[row + YH], at(dz=-1))
                if hop < 3:
                    act_z[hop, k].start()
                    started.append(act_z[hop, k])
                else:
                    pl.when(there <= yh)(act_z[hop, k].start)
        if hop == 1:
            pass_on(own_act, *d_act)
        if hop == 2:
            pass_on(own_grd, *d_grd)

    for copy in pair_copies:
        copy.wait_recv()
    to_smem = pltpu.make_async_copy(pair_tiles, pair_smem, local_sem.at[0])
    to_smem.start()
    to_smem.wait()

    def deliver(far, st, b):
        for j in range(GROUP):
            st[j] = far[yh + pair_smem[j, 0, 0]]
        copies = [send(st.at[in_group(*o)], b.at[tensor], (dp, in_group(*o))) for o in peers]
        b[tensor] = st[tensor]
        return copies

    for k in range(YH):
        there = (yh - k + YH) % YH
        pl.when(there <= yh)(act_z[3, k].wait_recv)
    e_act = deliver(far_act, st_act, b_act)
    for k in (1, 2, 3):
        there = (yh - k + YH) % YH
        pl.when(yh < there)(grd_y[0, k].wait_recv)
        for hop in (1, 2, 3):
            grd_y[hop, k].wait_recv()
        pl.when(yh > there)(grd_y[4, k].wait_recv)
    e_grd = deliver(far_grd, st_grd, b_grd)

    diagonal = (distance == DP // 2) & (dp >= DP // 2)
    is_diagonal = jnp.full((1, 1), jnp.where(diagonal, 1, 0), i32) == 1

    def tile(own, b, second, delivered, out, sem):
        for copy in second:
            copy.wait_recv()
        for copy in delivered:
            copy.wait_recv()
        left = unfold(own[...].reshape(GROUP * piece, own.shape[2]))
        far = unfold(b[...].reshape(GROUP * piece, b.shape[2]))
        right = jnp.where(jnp.broadcast_to(is_diagonal, far.shape), left, far)
        dims = (((0,), (0,)), ((), ()))
        upper = lax.dot_general(left, right, dims, preferred_element_type=f32)
        lower = lax.dot_general(far, far, dims, preferred_element_type=f32)
        p = lax.broadcasted_iota(i32, upper.shape, 0)
        q = lax.broadcasted_iota(i32, upper.shape, 1)
        take_lower = jnp.where(p > q, jnp.where(is_diagonal, 1, 0), 0) == 1
        sem[...] = jnp.where(take_lower, lower, upper) * (1.0 / (DP * 16))

    tile(own_act, b_act, d_act[1], e_act, None, tile_act)
    write_act = pltpu.make_async_copy(tile_act, act_out.at[0], local_sem.at[1])
    write_act.start()
    tile(own_grd, b_grd, d_grd[1], e_grd, None, tile_grd)
    write_grd = pltpu.make_async_copy(tile_grd, grad_out.at[0], local_sem.at[2])
    write_grd.start()

    for copy in started:
        copy.wait_send()
    for k in (1, 2, 3):
        pl.when((yh + k) % YH < yh)(grd_y[0, k].wait_send)
        pl.when((yh + k) % YH > yh)(grd_y[4, k].wait_send)
    for k in range(YH):
        pl.when((yh - k + YH) % YH <= yh)(act_z[3, k].wait_send)
    write_act.wait()
    write_grd.wait()


def local(tokens, out_grad, gate_weight, up_weight, down_weight, pair_list):
    rows, depth = tokens.shape
    width = gate_weight.shape[1]
    half = rows * DP // 4
    piece = half // CHIPS
    any_space = pl.BlockSpec(memory_space=pl.ANY)
    tile = jax.ShapeDtypeStruct((1, width, width), f32)

    def vmem(shape, kind):
        return pltpu.VMEM(shape, kind)

    scratch = [
        vmem((DP, rows, depth), bf16), vmem((DP, rows, depth), bf16),
        vmem((depth, width), bf16), vmem((depth, width), bf16), vmem((width, depth), bf16),
        vmem((GROUP, 8, 128), i32), pltpu.SMEM((GROUP, 8, 128), i32),
        vmem((2, half, 2 * width), f32), vmem((2, half, 2 * width), f32),
        vmem((1, half, 2 * width), f32), vmem((1, half, 2 * width), f32),
        vmem((2, half, 2 * width), f32), vmem((1, half, 2 * width), f32),
        vmem((CHIPS, 2, piece, 2 * width), i16), vmem((CHIPS - 1, 2, piece, 2 * width), i16),
        vmem((CHIPS, 1, piece, 2 * width), i16), vmem((CHIPS - 1, 1, piece, 2 * width), i16),
        vmem((2, 8, 128), f32), vmem((CHIPS - 1, 2, 8, 128), f32),
        vmem((1, 8, 128), f32), vmem((CHIPS - 1, 1, 8, 128), f32),
        vmem((GROUP, piece, 2 * width), bf16), vmem((GROUP, piece, 2 * width), bf16),
        vmem((5 * YH, piece, 2 * width), bf16), vmem((5 * YH, piece, 2 * width), bf16),
        vmem((GROUP, piece, 2 * width), bf16), vmem((GROUP, piece, 2 * width), bf16),
        vmem((GROUP, piece, 2 * width), bf16), vmem((GROUP, piece, 2 * width), bf16),
        vmem((width, width), f32), vmem((width, width), f32),
        pltpu.SemaphoreType.DMA((5,)), pltpu.SemaphoreType.DMA((200,)), pltpu.SemaphoreType.DMA((200,)),
    ]
    return pl.pallas_call(
        kernel,
        out_shape=(tile, tile),
        in_specs=[any_space] * 5 + [pl.BlockSpec(memory_space=pltpu.SMEM)],
        out_specs=(any_space, any_space),
        scratch_shapes=scratch,
        compiler_params=pltpu.CompilerParams(
            collective_id=0, has_side_effects=True, vmem_limit_bytes=48 * 1024 * 1024),
        name="covariance",
    )(tokens, out_grad, gate_weight, up_weight, down_weight, pair_list)


def solution(mesh):
    in_specs = (
        P("dp", "tensor"),
        P("dp", "tensor"),
        P("tensor", "dp"),
        P("tensor", "dp"),
        P("dp", "tensor"),
        P(("dp", "tensor"), None),
    )
    out_specs = (P(("dp", "tensor"), None, None), P(("dp", "tensor"), None, None))
    return jax.shard_map(local, mesh=mesh, in_specs=in_specs, out_specs=out_specs, check_vma=False)
```

```python
import jax
import jax.numpy as jnp
from jax import lax
from jax.experimental import pallas as pl
from jax.experimental.pallas import tpu as pltpu
from jax.sharding import PartitionSpec as P

Z, YH, X, YL, CORES = 8, 4, 4, 2, 2
DP, GROUP = Z * YH, X * YL * CORES
CHIPS = X * YL
LEVELS = 32760.0
MESH = pl.DeviceIdType.MESH
f32, bf16, i16, i32 = jnp.float32, jnp.bfloat16, jnp.int16, jnp.int32


def encode(value, largest):
    root = jnp.sqrt(jnp.abs(value)) * (LEVELS * lax.rsqrt(largest))
    code = (root + 0.5).astype(i32)
    return jnp.where(value < 0, -code, code).astype(i16)


def decode(code, unit):
    root = code.astype(i32).astype(f32)
    return root * jnp.abs(root) * unit


def fold(rows):
    half = rows.shape[0] // 2
    return jnp.concatenate([rows[:half], rows[half:]], axis=1)


def unfold(folded):
    width = folded.shape[1] // 2
    return jnp.concatenate([folded[:, :width], folded[:, width:]], axis=0)


def kernel(tok_in, grd_in, wg_in, wu_in, wd_in, pair, act_out, grad_out,
           x_tok, x_grd, wg, wu, wd, pair_tiles, pair_smem,
           ps_act, pr_act, ps_grd, pr_grd, sum_act, sum_grd,
           cs_act, cr_act, cs_grd, cr_grd, us_act, ur_act, us_grd, ur_grd,
           own_act, own_grd, far_act, far_grd, pass_act, pass_grd, st_act, st_grd, b_act, b_grd,
           tile_act, tile_grd, local_sem, send_sem, recv_sem):
    dp, tensor = lax.axis_index("dp"), lax.axis_index("tensor")
    z, yh = dp // YH, dp % YH
    core, chip = tensor % CORES, tensor // CORES
    x, yl = chip // YL, chip % YL

    def at(dz=0, dyh=0):
        return ((z + dz + Z) % Z * YH + (yh + dyh + YH) % YH, tensor)

    def in_group(dx, dyl, dc, sign=1):
        return (((x + sign * dx + X) % X * YL + (yl + dyl) % YL) * CORES + (core + dc) % CORES)

    used = [0]
    sent = []

    def send(src, dst, device, only=None):
        n = used[0]
        used[0] += 1
        copy = pltpu.make_async_remote_copy(
            src_ref=src, dst_ref=dst, send_sem=send_sem.at[n], recv_sem=recv_sem.at[n],
            device_id=device, device_id_type=MESH)
        if only is None:
            copy.start()
        else:
            pl.when(only)(copy.start)
        sent.append((only, copy))
        return copy

    peers = [(dx, dyl, dc) for dx in (2, 1, 3, 0) for dyl in (1, 0) for dc in (0, 1) if (dx, dyl, dc) != (0, 0, 0)]
    chip_peers = [(dx, dyl) for dx in (2, 1, 3, 0) for dyl in (1, 0) if (dx, dyl) != (0, 0)]

    barrier = pltpu.get_barrier_semaphore()
    partners = [at(dyh=k) for k in (1, 2, 3)] + [at(dz=k) for k in (1, -1, 2, -2)] + [(dp, in_group(*o)) for o in peers]
    for partner in partners:
        pl.semaphore_signal(barrier, inc=1, device_id=partner, device_id_type=MESH)
    loads = [pltpu.make_async_copy(tok_in, x_tok.at[dp], local_sem.at[0]),
             pltpu.make_async_copy(grd_in, x_grd.at[dp], local_sem.at[1]),
             pltpu.make_async_copy(wg_in, wg, local_sem.at[2]),
             pltpu.make_async_copy(wu_in, wu, local_sem.at[3]),
             pltpu.make_async_copy(wd_in, wd, local_sem.at[4])]
    for load in loads:
        load.start()
    distance = (pair[0, 1] - pair[0, 0] + DP) % DP
    pair_tiles[tensor] = jnp.full((8, 128), distance, i32)
    pl.semaphore_wait(barrier, len(partners))

    def y_slot(k):
        return (yh - k + YH) % YH

    ring = {}

    def along_z(b, buf, src, k):
        slot = z * YH + y_slot(k)
        for step in (2, 1):
            for way in (1, -1):
                ring[b, way, step, k] = send(src, buf.at[slot], at(dz=way * step))

    def pass_along_z(b, buf, k):
        for way in (1, -1):
            ring[b, way, 2, k].wait_recv()
            slot = (z - way * 2 + Z) % Z * YH + y_slot(k)
            if (way == 1) == (k in (0, 2)):
                ring[b, way, 4, k] = send(buf.at[slot], buf.at[slot], at(dz=way * 2))
            ring[b, way, 3, k] = send(buf.at[slot], buf.at[slot], at(dz=way))

    def all_rows(b, pieces):
        for k in pieces:
            for way in (1, -1):
                if b == 1 or k != 0:
                    ring[b, way, 1, k].wait_recv()
                    ring[b, way, 3, k].wait_recv()
                    if (b, way, 4, k) in ring:
                        ring[b, way, 4, k].wait_recv()

    y_tok = {}
    y_tok[0, 2] = send(tok_in, x_tok.at[dp], at(dyh=2))
    along_z(0, x_tok, tok_in, 0)
    for k in (1, 3):
        y_tok[0, k] = send(tok_in, x_tok.at[dp], at(dyh=k))
    y_grd = {k: send(grd_in, x_grd.at[dp], at(dyh=k)) for k in (2, 1, 3)}

    def to_neighbours(shift):
        slot = (z - shift + Z) % Z * YH + yh
        for k in (1, 3):
            y_tok[shift, k] = send(x_tok.at[slot], x_tok.at[slot], at(dyh=k))

    for way in (1, -1):
        ring[0, way, 1, 0].wait_recv()
        to_neighbours(way)
    pass_along_z(0, x_tok, 0)
    to_neighbours(2)
    to_neighbours(-2)
    y_tok[0, 2].wait_recv()
    along_z(0, x_tok, x_tok.at[z * YH + y_slot(2)], 2)
    along_z(1, x_grd, grd_in, 0)
    for way in (1, -1):
        ring[0, way, 3, 0].wait_recv()
        to_neighbours(way * 3)
    ring[0, 1, 4, 0].wait_recv()
    to_neighbours(4)
    pass_along_z(0, x_tok, 2)
    for k in (1, 3, 2):
        y_grd[k].wait_recv()
        along_z(1, x_grd, x_grd.at[z * YH + y_slot(k)], k)
    pair_copies = [send(pair_tiles.at[tensor], pair_tiles.at[tensor], (dp, in_group(*o))) for o in peers]
    for load in loads:
        load.wait()

    other = (dp, in_group(0, 0, 1))
    piece = cs_act.shape[2]

    def product(buf, half, weight):
        rows = buf[pl.ds(half * (DP // 2), DP // 2)].reshape(buf.shape[1] * DP // 2, buf.shape[2])
        return fold(lax.dot_general(rows, weight[...], (((1,), (1,)), ((), ())), preferred_element_type=f32))

    def for_other(buf, weights, ps, pr):
        pairs = []
        for i, weight in enumerate(weights):
            ps[i] = product(buf, 1 - core, weight)
            pairs.append(send(ps.at[i], pr.at[i], other))
        return pairs

    def rows_of_chip(q):
        return pl.ds(pl.multiple_of(q * piece, piece), piece)

    def spread(pairs, total, pr, cs, us, cr, ur):
        for pair_copy in pairs:
            pair_copy.wait_recv()
        copies = []
        for n, (dx, dyl) in enumerate(chip_peers):
            there = in_group(dx, dyl, 0)
            q = there // CORES
            for i in range(total.shape[0]):
                summed = total[i, rows_of_chip(q)] + pr[i, rows_of_chip(q)]
                most = jnp.maximum(jnp.max(jnp.abs(summed)), 1e-30)
                us[q, i] = jnp.full((8, 128), most * (1.0 / (LEVELS * LEVELS)), f32)
                cs[q, i] = encode(summed, most)
            copies.append((send(us.at[q], ur.at[n], (dp, there)), send(cs.at[q], cr.at[n], (dp, there))))
        return copies

    def gathered(copies, total, pr, cr, ur):
        mine = [total[i, rows_of_chip(chip)] + pr[i, rows_of_chip(chip)] for i in range(total.shape[0])]
        for n, copy in enumerate(copies):
            for c in copy:
                c.wait_recv()
            for i in range(total.shape[0]):
                mine[i] += decode(cr[n, i], ur[n, i, 0:1, 0:1])
        return mine

    all_rows(0, (2,))
    for shift in (0, 1, -1, 2, -2, 3, -3, 4):
        for k in (1, 3):
            y_tok[shift, k].wait_recv()
    pairs = for_other(x_tok, (wg, wu), ps_act, pr_act)
    for k in (0, 1, 3, 2):
        pass_along_z(1, x_grd, k)
    for i, weight in enumerate((wg, wu)):
        sum_act[i] = product(x_tok, core, weight)
    c_act = spread(pairs, sum_act, pr_act, cs_act, us_act, cr_act, ur_act)
    all_rows(1, range(YH))
    pairs = for_other(x_grd, (wd,), ps_grd, pr_grd)
    sum_grd[0] = product(x_grd, core, wd)
    c_grd = spread(pairs, sum_grd, pr_grd, cs_grd, us_grd, cr_grd, ur_grd)

    for copy in pair_copies:
        copy.wait_recv()
    to_smem = pltpu.make_async_copy(pair_tiles, pair_smem, local_sem.at[0])
    to_smem.start()
    to_smem.wait()

    far_x = (2, 1, 3)

    def share_out(own):
        across = send(own.at[tensor], own.at[tensor], (dp, in_group(0, 1, 0)))
        along = [send(own.at[tensor], own.at[tensor], (dp, in_group(dx, 0, 0))) for dx in far_x]
        return across, along, [send(own.at[tensor], own.at[tensor], other)]

    def pass_across(own, across, along, second):
        across.wait_recv()
        slot = in_group(0, 1, 0)
        along += [send(own.at[slot], own.at[slot], (dp, in_group(dx, 0, 0))) for dx in far_x]
        second.append(send(own.at[slot], own.at[slot], other))

    def pass_on(own, across, along, second):
        for n, copy in enumerate(along):
            copy.wait_recv()
            slot = in_group(far_x[n % 3], n // 3, 0, sign=-1)
            second.append(send(own.at[slot], own.at[slot], other))

    def down_z(far, through, k, e_z):
        slot = y_slot(k)
        e_z[2, k] = send(far.at[slot], far.at[2 * YH + slot], at(dz=-2))
        e_z[-2, k] = send(far.at[slot], through.at[slot], at(dz=2), None if k == 0 else slot <= yh)
        e_z[1, k] = send(far.at[slot], far.at[YH + slot], at(dz=-1))

    def pass_down_z(far, through, k, e_z):
        slot = y_slot(k)
        e_z[2, k].wait_recv()
        e_z[3, k] = send(far.at[2 * YH + slot], far.at[3 * YH + slot], at(dz=-1))
        if k == 0:
            e_z[-2, k].wait_recv()
            e_z[4, k] = send(through.at[slot], far.at[4 * YH + slot], at(dz=2))
        else:
            pl.when(slot <= yh)(e_z[-2, k].wait_recv)
            e_z[4, k] = send(through.at[slot], far.at[4 * YH + slot], at(dz=2), slot <= yh)

    gate, up = gathered(c_act, sum_act, pr_act, cr_act, ur_act)
    hidden = (gate / (1.0 + jnp.exp(-gate)) * up).astype(bf16)
    own_act[tensor] = hidden
    far_act[yh] = hidden
    act_y = {k: send(far_act.at[yh], far_act.at[yh], at(dyh=k)) for k in (2, 1, 3)}
    act_z = {}
    down_z(far_act, pass_act, 0, act_z)
    d_act = share_out(own_act)

    (grad_sum,) = gathered(c_grd, sum_grd, pr_grd, cr_grd, ur_grd)
    hidden_grad = grad_sum.astype(bf16)
    own_grd[tensor] = hidden_grad
    far_grd[yh] = hidden_grad
    grd_z, grd_y = {}, {}
    down_z(far_grd, pass_grd, 0, grd_z)
    for k in (2, 1, 3):
        grd_y[0, k] = send(far_grd.at[yh], far_grd.at[yh], at(dyh=k), (yh + k) % YH < yh)
    d_grd = share_out(own_grd)

    def over_y(hop):
        slot = hop * YH + yh
        for k in (2, 1, 3):
            grd_y[hop, k] = send(far_grd.at[slot], far_grd.at[slot], at(dyh=k), None if hop < 4 else (yh + k) % YH > yh)

    pass_down_z(far_act, pass_act, 0, act_z)
    for k in (1, 3, 2):
        act_y[k].wait_recv()
        down_z(far_act, pass_act, k, act_z)
    grd_z[1, 0].wait_recv()
    over_y(1)
    pass_down_z(far_grd, pass_grd, 0, grd_z)
    over_y(2)
    pass_across(own_act, *d_act)
    pass_across(own_grd, *d_grd)
    for k in (1, 3, 2):
        pass_down_z(far_act, pass_act, k, act_z)
    for hop in (3, 4):
        grd_z[hop, 0].wait_recv()
        over_y(hop)
    pass_on(own_act, *d_act)
    pass_on(own_grd, *d_grd)

    def deliver(far, st, b):
        for j in range(GROUP):
            st[j] = far[yh + pair_smem[j, 0, 0]]
        copies = [send(st.at[in_group(*o)], b.at[tensor], (dp, in_group(*o))) for o in peers]
        b[tensor] = st[tensor]
        return copies

    for k in range(YH):
        act_z[1, k].wait_recv()
        act_z[3, k].wait_recv()
        if k == 0:
            act_z[4, k].wait_recv()
        else:
            pl.when(y_slot(k) <= yh)(act_z[4, k].wait_recv)
    e_act = deliver(far_act, st_act, b_act)
    for k in (1, 2, 3):
        there = y_slot(k)
        pl.when(yh < there)(grd_y[0, k].wait_recv)
        for hop in (1, 2, 3):
            grd_y[hop, k].wait_recv()
        pl.when(yh > there)(grd_y[4, k].wait_recv)
    e_grd = deliver(far_grd, st_grd, b_grd)

    diagonal = (distance == DP // 2) & (dp >= DP // 2)
    is_diagonal = jnp.full((1, 1), jnp.where(diagonal, 1, 0), i32) == 1

    def tile(own, b, second, delivered, out):
        for copy in second + delivered:
            copy.wait_recv()
        left = unfold(own[...].reshape(GROUP * piece, own.shape[2]))
        far = unfold(b[...].reshape(GROUP * piece, b.shape[2]))
        right = jnp.where(jnp.broadcast_to(is_diagonal, far.shape), left, far)
        dims = (((0,), (0,)), ((), ()))
        upper = lax.dot_general(left, right, dims, preferred_element_type=f32)
        lower = lax.dot_general(far, far, dims, preferred_element_type=f32)
        p = lax.broadcasted_iota(i32, upper.shape, 0)
        q = lax.broadcasted_iota(i32, upper.shape, 1)
        take_lower = jnp.where(p > q, jnp.where(is_diagonal, 1, 0), 0) == 1
        out[...] = jnp.where(take_lower, lower, upper) * (1.0 / (DP * 16))

    tile(own_act, b_act, d_act[2], e_act, tile_act)
    write_act = pltpu.make_async_copy(tile_act, act_out.at[0], local_sem.at[1])
    write_act.start()
    tile(own_grd, b_grd, d_grd[2], e_grd, tile_grd)
    write_grd = pltpu.make_async_copy(tile_grd, grad_out.at[0], local_sem.at[2])
    write_grd.start()

    for only, copy in sent:
        if only is None:
            copy.wait_send()
        else:
            pl.when(only)(copy.wait_send)
    write_act.wait()
    write_grd.wait()


def local(tokens, out_grad, gate_weight, up_weight, down_weight, pair_list):
    rows, depth = tokens.shape
    width = gate_weight.shape[1]
    half = rows * DP // 4
    piece = half // CHIPS
    any_space = pl.BlockSpec(memory_space=pl.ANY)
    tile = jax.ShapeDtypeStruct((1, width, width), f32)

    def vmem(shape, kind):
        return pltpu.VMEM(shape, kind)

    scratch = [
        vmem((DP, rows, depth), bf16), vmem((DP, rows, depth), bf16),
        vmem((width, depth), bf16), vmem((width, depth), bf16), vmem((width, depth), bf16),
        vmem((GROUP, 8, 128), i32), pltpu.SMEM((GROUP, 8, 128), i32),
        vmem((2, half, 2 * width), f32), vmem((2, half, 2 * width), f32),
        vmem((1, half, 2 * width), f32), vmem((1, half, 2 * width), f32),
        vmem((2, half, 2 * width), f32), vmem((1, half, 2 * width), f32),
        vmem((CHIPS, 2, piece, 2 * width), i16), vmem((CHIPS - 1, 2, piece, 2 * width), i16),
        vmem((CHIPS, 1, piece, 2 * width), i16), vmem((CHIPS - 1, 1, piece, 2 * width), i16),
        vmem((CHIPS, 2, 8, 128), f32), vmem((CHIPS - 1, 2, 8, 128), f32),
        vmem((CHIPS, 1, 8, 128), f32), vmem((CHIPS - 1, 1, 8, 128), f32),
        vmem((GROUP, piece, 2 * width), bf16), vmem((GROUP, piece, 2 * width), bf16),
        vmem((5 * YH, piece, 2 * width), bf16), vmem((5 * YH, piece, 2 * width), bf16),
        vmem((YH, piece, 2 * width), bf16), vmem((YH, piece, 2 * width), bf16),
        vmem((GROUP, piece, 2 * width), bf16), vmem((GROUP, piece, 2 * width), bf16),
        vmem((GROUP, piece, 2 * width), bf16), vmem((GROUP, piece, 2 * width), bf16),
        vmem((width, width), f32), vmem((width, width), f32),
        pltpu.SemaphoreType.DMA((5,)), pltpu.SemaphoreType.DMA((256,)), pltpu.SemaphoreType.DMA((256,)),
    ]
    return pl.pallas_call(
        kernel,
        out_shape=(tile, tile),
        in_specs=[any_space] * 5 + [pl.BlockSpec(memory_space=pltpu.SMEM)],
        out_specs=(any_space, any_space),
        scratch_shapes=scratch,
        compiler_params=pltpu.CompilerParams(
            collective_id=0, has_side_effects=True, vmem_limit_bytes=60 * 1024 * 1024),
        name="covariance",
    )(tokens, out_grad, gate_weight.T, up_weight.T, down_weight, pair_list)


def solution(mesh):
    in_specs = (
        P("dp", "tensor"),
        P("dp", "tensor"),
        P("tensor", "dp"),
        P("tensor", "dp"),
        P("dp", "tensor"),
        P(("dp", "tensor"), None),
    )
    out_specs = (P(("dp", "tensor"), None, None), P(("dp", "tensor"), None, None))
    return jax.shard_map(local, mesh=mesh, in_specs=in_specs, out_specs=out_specs, check_vma=False)
```

```python
import jax
import jax.numpy as jnp
from jax import lax
from jax.experimental import pallas as pl
from jax.experimental.pallas import tpu as pltpu
from jax.sharding import PartitionSpec as P

Z, YH, X, YL, CORES = 8, 4, 4, 2, 2
DP, GROUP = Z * YH, X * YL * CORES
CHIPS = X * YL
LEVELS = 32760.0
MESH = pl.DeviceIdType.MESH
f32, bf16, i16, i32 = jnp.float32, jnp.bfloat16, jnp.int16, jnp.int32


def encode(value, largest):
    root = jnp.sqrt(jnp.abs(value)) * (LEVELS * lax.rsqrt(largest))
    code = (root + 0.5).astype(i32)
    return jnp.where(value < 0, -code, code).astype(i16)


def decode(code, unit):
    root = code.astype(i32).astype(f32)
    return root * jnp.abs(root) * unit


def fold(rows):
    half = rows.shape[0] // 2
    return jnp.concatenate([rows[:half], rows[half:]], axis=1)


def unfold(folded):
    width = folded.shape[1] // 2
    return jnp.concatenate([folded[:, :width], folded[:, width:]], axis=0)


def kernel(tok_in, grd_in, wg_in, wu_in, wd_in, pair, act_out, grad_out,
           x_tok, x_grd, wg, wu, wd, pair_tiles, pair_smem,
           ps_act, pr_act, ps_grd, pr_grd, sum_act, sum_grd,
           cs_act, cr_act, cs_grd, cr_grd, us_act, ur_act, us_grd, ur_grd,
           own_act, own_grd, far_act, far_grd, pass_grd, st_act, st_grd, b_act, b_grd,
           tile_act, tile_grd, local_sem, send_sem, recv_sem):
    dp, tensor = lax.axis_index("dp"), lax.axis_index("tensor")
    z, yh = dp // YH, dp % YH
    core, chip = tensor % CORES, tensor // CORES
    x, yl = chip // YL, chip % YL

    def at(dz=0, dyh=0):
        return ((z + dz + Z) % Z * YH + (yh + dyh + YH) % YH, tensor)

    def in_group(dx, dyl, dc, sign=1):
        return (((x + sign * dx + X) % X * YL + (yl + dyl) % YL) * CORES + (core + dc) % CORES)

    used = [0]
    sent = []

    def send(src, dst, device, only=None):
        n = used[0]
        used[0] += 1
        copy = pltpu.make_async_remote_copy(
            src_ref=src, dst_ref=dst, send_sem=send_sem.at[n], recv_sem=recv_sem.at[n],
            device_id=device, device_id_type=MESH)
        if only is None:
            copy.start()
        else:
            pl.when(only)(copy.start)
        sent.append((only, copy))
        return copy

    peers = [(dx, dyl, dc) for dx in (2, 1, 3, 0) for dyl in (1, 0) for dc in (0, 1) if (dx, dyl, dc) != (0, 0, 0)]
    chip_peers = [(dx, dyl) for dx in (2, 1, 3, 0) for dyl in (1, 0) if (dx, dyl) != (0, 0)]

    barrier = pltpu.get_barrier_semaphore()
    partners = [at(dyh=k) for k in (1, 2, 3)] + [at(dz=k) for k in (1, -1, 2, -2, 3, -3, 4)] + [(dp, in_group(*o)) for o in peers]
    for partner in partners:
        pl.semaphore_signal(barrier, inc=1, device_id=partner, device_id_type=MESH)
    loads = [pltpu.make_async_copy(tok_in, x_tok.at[dp], local_sem.at[0]),
             pltpu.make_async_copy(grd_in, x_grd.at[dp], local_sem.at[1]),
             pltpu.make_async_copy(wg_in, wg, local_sem.at[2]),
             pltpu.make_async_copy(wu_in, wu, local_sem.at[3]),
             pltpu.make_async_copy(wd_in, wd, local_sem.at[4])]
    for load in loads:
        load.start()
    distance = (pair[0, 1] - pair[0, 0] + DP) % DP
    pair_tiles[tensor] = jnp.full((8, 128), distance, i32)
    pl.semaphore_wait(barrier, len(partners))

    def y_slot(k):
        return (yh - k + YH) % YH

    ring = {}

    def along_z(b, buf, src, k):
        slot = z * YH + y_slot(k)
        for step in (2, 1):
            for way in (1, -1):
                ring[b, way, step, k] = send(src, buf.at[slot], at(dz=way * step))

    def pass_along_z(b, buf, k):
        for way in (1, -1):
            ring[b, way, 2, k].wait_recv()
            slot = (z - way * 2 + Z) % Z * YH + y_slot(k)
            if (way == 1) == (k in (0, 2)):
                ring[b, way, 4, k] = send(buf.at[slot], buf.at[slot], at(dz=way * 2))
            ring[b, way, 3, k] = send(buf.at[slot], buf.at[slot], at(dz=way))

    def all_rows(b):
        for k in range(YH):
            for way in (1, -1):
                ring[b, way, 1, k].wait_recv()
                ring[b, way, 3, k].wait_recv()
                if (b, way, 4, k) in ring:
                    ring[b, way, 4, k].wait_recv()

    y_tok = {}
    shifts = (4, 3, -3, 2, -2, 1, -1)
    z_tok = {}

    def to_all_z(src, k):
        slot = z * YH + y_slot(k)
        for shift in shifts:
            z_tok[shift, k] = send(src, x_tok.at[slot], at(dz=shift))

    y_tok[0, 2] = send(tok_in, x_tok.at[dp], at(dyh=2))
    to_all_z(tok_in, 0)
    for k in (1, 3):
        y_tok[0, k] = send(tok_in, x_tok.at[dp], at(dyh=k))
    y_grd = {k: send(grd_in, x_grd.at[dp], at(dyh=k)) for k in (2, 1, 3)}

    def to_neighbours(shift):
        slot = (z - shift + Z) % Z * YH + yh
        for k in (1, 3):
            y_tok[shift, k] = send(x_tok.at[slot], x_tok.at[slot], at(dyh=k))

    for shift in (1, -1, 2, -2):
        z_tok[shift, 0].wait_recv()
        to_neighbours(shift)
    y_tok[0, 2].wait_recv()
    to_all_z(x_tok.at[z * YH + y_slot(2)], 2)
    for shift in (3, -3, 4):
        z_tok[shift, 0].wait_recv()
        to_neighbours(shift)
    along_z(1, x_grd, grd_in, 0)
    for k in (1, 3, 2):
        y_grd[k].wait_recv()
        along_z(1, x_grd, x_grd.at[z * YH + y_slot(k)], k)
    pair_copies = [send(pair_tiles.at[tensor], pair_tiles.at[tensor], (dp, in_group(*o))) for o in peers]
    for load in loads:
        load.wait()

    other = (dp, in_group(0, 0, 1))
    piece = cs_act.shape[2]

    def product(buf, half, weight):
        rows = buf[pl.ds(half * (DP // 2), DP // 2)].reshape(buf.shape[1] * DP // 2, buf.shape[2])
        return fold(lax.dot_general(rows, weight[...], (((1,), (1,)), ((), ())), preferred_element_type=f32))

    def for_other(buf, weights, ps, pr):
        pairs = []
        for i, weight in enumerate(weights):
            ps[i] = product(buf, 1 - core, weight)
            pairs.append(send(ps.at[i], pr.at[i], other))
        return pairs

    def rows_of_chip(q):
        return pl.ds(pl.multiple_of(q * piece, piece), piece)

    def spread(pairs, total, pr, cs, us, cr, ur):
        for pair_copy in pairs:
            pair_copy.wait_recv()
        largest = {}
        for dx, dyl in chip_peers:
            q = in_group(dx, dyl, 0) // CORES
            for i in range(total.shape[0]):
                summed = total[i, rows_of_chip(q)] + pr[i, rows_of_chip(q)]
                total[i, rows_of_chip(q)] = summed
                most = jnp.max(jnp.max(jnp.abs(summed), axis=0, keepdims=True), axis=1, keepdims=True)
                largest[dx, dyl, i] = jnp.maximum(most, 1e-30)
        copies = []
        for n, (dx, dyl) in enumerate(chip_peers):
            there = in_group(dx, dyl, 0)
            q = there // CORES
            for i in range(total.shape[0]):
                most = largest[dx, dyl, i]
                us[q, i] = jnp.broadcast_to(most * (1.0 / (LEVELS * LEVELS)), (8, 128))
                cs[q, i] = encode(total[i, rows_of_chip(q)], most)
            copies.append((send(us.at[q], ur.at[n], (dp, there)), send(cs.at[q], cr.at[n], (dp, there))))
        return copies

    def gathered(copies, total, pr, cr, ur):
        mine = [total[i, rows_of_chip(chip)] + pr[i, rows_of_chip(chip)] for i in range(total.shape[0])]
        for n, copy in enumerate(copies):
            for c in copy:
                c.wait_recv()
            for i in range(total.shape[0]):
                mine[i] += decode(cr[n, i], ur[n, i, 0:1, 0:1])
        return mine

    for shift in reversed(shifts):
        z_tok[shift, 2].wait_recv()
    for shift in (0, 1, -1, 2, -2, 3, -3, 4):
        for k in (1, 3):
            y_tok[shift, k].wait_recv()
    pairs = for_other(x_tok, (wg, wu), ps_act, pr_act)
    for k in (0, 1, 3, 2):
        pass_along_z(1, x_grd, k)
    for i, weight in enumerate((wg, wu)):
        sum_act[i] = product(x_tok, core, weight)
    c_act = spread(pairs, sum_act, pr_act, cs_act, us_act, cr_act, ur_act)
    all_rows(1)
    pairs = for_other(x_grd, (wd,), ps_grd, pr_grd)
    sum_grd[0] = product(x_grd, core, wd)
    c_grd = spread(pairs, sum_grd, pr_grd, cs_grd, us_grd, cr_grd, ur_grd)

    for copy in pair_copies:
        copy.wait_recv()
    to_smem = pltpu.make_async_copy(pair_tiles, pair_smem, local_sem.at[0])
    to_smem.start()
    to_smem.wait()

    far_x = (2, 1, 3)

    def share_out(own):
        across = send(own.at[tensor], own.at[tensor], (dp, in_group(0, 1, 0)))
        along = [send(own.at[tensor], own.at[tensor], (dp, in_group(dx, 0, 0))) for dx in far_x]
        return across, along, [send(own.at[tensor], own.at[tensor], other)]

    def pass_across(own, across, along, second):
        across.wait_recv()
        slot = in_group(0, 1, 0)
        along += [send(own.at[slot], own.at[slot], (dp, in_group(dx, 0, 0))) for dx in far_x]
        second.append(send(own.at[slot], own.at[slot], other))

    def pass_on(own, across, along, second):
        for n, copy in enumerate(along):
            copy.wait_recv()
            slot = in_group(far_x[n % 3], n // 3, 0, sign=-1)
            second.append(send(own.at[slot], own.at[slot], other))

    def straight_down(far, k, e_z):
        slot = y_slot(k)
        for d in (4, 3, 2, 1):
            e_z[d, k] = send(far.at[slot], far.at[d * YH + slot], at(dz=-d), None if d < 4 or k == 0 else slot <= yh)

    def over_y(far, e_y, hop):
        slot = hop * YH + yh
        for k in (1, 3):
            only = {0: (yh + k) % YH < yh, 4: (yh + k) % YH > yh}.get(hop)
            e_y[hop, k] = send(far.at[slot], far.at[slot], at(dyh=k), only)

    def down_z(far, through, k, e_z):
        slot = y_slot(k)
        e_z[2, k] = send(far.at[slot], far.at[2 * YH + slot], at(dz=-2))
        e_z[-2, k] = send(far.at[slot], through.at[slot], at(dz=2), None if k == 0 else slot <= yh)
        e_z[1, k] = send(far.at[slot], far.at[YH + slot], at(dz=-1))

    def pass_down_z(far, through, k, e_z):
        slot = y_slot(k)
        e_z[2, k].wait_recv()
        e_z[3, k] = send(far.at[2 * YH + slot], far.at[3 * YH + slot], at(dz=-1))
        if k == 0:
            e_z[-2, k].wait_recv()
            e_z[4, k] = send(through.at[slot], far.at[4 * YH + slot], at(dz=2))
        else:
            pl.when(slot <= yh)(e_z[-2, k].wait_recv)
            e_z[4, k] = send(through.at[slot], far.at[4 * YH + slot], at(dz=2), slot <= yh)

    gate, up = gathered(c_act, sum_act, pr_act, cr_act, ur_act)
    hidden = (gate / (1.0 + jnp.exp(-gate)) * up).astype(bf16)
    own_act[tensor] = hidden
    far_act[yh] = hidden
    act_z, act_y = {}, {}
    act_opposite = send(far_act.at[yh], far_act.at[yh], at(dyh=2))
    straight_down(far_act, 0, act_z)
    over_y(far_act, act_y, 0)
    d_act = share_out(own_act)

    (grad_sum,) = gathered(c_grd, sum_grd, pr_grd, cr_grd, ur_grd)
    hidden_grad = grad_sum.astype(bf16)
    own_grd[tensor] = hidden_grad
    far_grd[yh] = hidden_grad
    grd_z, grd_y = {}, {}
    grd_opposite = send(far_grd.at[yh], far_grd.at[yh], at(dyh=2))
    down_z(far_grd, pass_grd, 0, grd_z)
    over_y(far_grd, grd_y, 0)
    d_grd = share_out(own_grd)

    for hop in (1, 2):
        act_z[hop, 0].wait_recv()
        over_y(far_act, act_y, hop)
    act_opposite.wait_recv()
    straight_down(far_act, 2, act_z)
    for hop in (3, 4):
        act_z[hop, 0].wait_recv()
        over_y(far_act, act_y, hop)
    grd_z[1, 0].wait_recv()
    over_y(far_grd, grd_y, 1)
    pass_down_z(far_grd, pass_grd, 0, grd_z)
    over_y(far_grd, grd_y, 2)
    grd_opposite.wait_recv()
    down_z(far_grd, pass_grd, 2, grd_z)
    pass_across(own_act, *d_act)
    pass_across(own_grd, *d_grd)
    for hop in (3, 4):
        grd_z[hop, 0].wait_recv()
        over_y(far_grd, grd_y, hop)
    pass_down_z(far_grd, pass_grd, 2, grd_z)
    pass_on(own_act, *d_act)

    def deliver(far, st, b):
        for j in range(GROUP):
            st[j] = far[yh + pair_smem[j, 0, 0]]
        copies = [send(st.at[in_group(*o)], b.at[tensor], (dp, in_group(*o))) for o in peers]
        b[tensor] = st[tensor]
        return copies

    def all_far(e_z, e_y, steps):
        for step in steps:
            e_z[step, 2].wait_recv()
        pl.when(y_slot(2) <= yh)(e_z[4, 2].wait_recv)
        for k in (1, 3):
            there = y_slot(k)
            pl.when(yh < there)(e_y[0, k].wait_recv)
            for hop in (1, 2, 3):
                e_y[hop, k].wait_recv()
            pl.when(yh > there)(e_y[4, k].wait_recv)

    all_far(act_z, act_y, (1, 2, 3))
    before = len(sent)
    e_act = deliver(far_act, st_act, b_act)
    pass_on(own_grd, *d_grd)
    all_far(grd_z, grd_y, (1, 3))
    e_grd = deliver(far_grd, st_grd, b_grd)

    diagonal = (distance == DP // 2) & (dp >= DP // 2)
    is_diagonal = jnp.full((1, 1), jnp.where(diagonal, 1, 0), i32) == 1

    def tile(own, b, second, delivered, out):
        for copy in second + delivered:
            copy.wait_recv()
        left = unfold(own[...].reshape(GROUP * piece, own.shape[2]))
        far = unfold(b[...].reshape(GROUP * piece, b.shape[2]))
        right = jnp.where(jnp.broadcast_to(is_diagonal, far.shape), left, far)
        dims = (((0,), (0,)), ((), ()))
        upper = lax.dot_general(left, right, dims, preferred_element_type=f32)
        lower = lax.dot_general(far, far, dims, preferred_element_type=f32)
        p = lax.broadcasted_iota(i32, upper.shape, 0)
        q = lax.broadcasted_iota(i32, upper.shape, 1)
        take_lower = jnp.where(p > q, jnp.where(is_diagonal, 1, 0), 0) == 1
        out[...] = jnp.where(take_lower, lower, upper) * (1.0 / (DP * 16))

    def finish(copies):
        for only, copy in copies:
            if only is None:
                copy.wait_send()
            else:
                pl.when(only)(copy.wait_send)

    finish(sent[:before])
    tile(own_act, b_act, d_act[2], e_act, tile_act)
    write_act = pltpu.make_async_copy(tile_act, act_out.at[0], local_sem.at[1])
    write_act.start()
    tile(own_grd, b_grd, d_grd[2], e_grd, tile_grd)
    write_grd = pltpu.make_async_copy(tile_grd, grad_out.at[0], local_sem.at[2])
    write_grd.start()

    finish(sent[before:])
    write_act.wait()
    write_grd.wait()


def hand_over(act, grad, act_out, grad_out, held, load_sems, store_sems):
    parts, rows = held.shape[1], held.shape[2]
    loads, stores = [], []
    for i, (source, target) in enumerate(((act, act_out), (grad, grad_out))):
        for n in range(parts):
            part = pl.ds(n * rows, rows)
            loads.append(pltpu.make_async_copy(source.at[0, part], held.at[i, n], load_sems.at[i, n]))
            stores.append(pltpu.make_async_copy(held.at[i, n], target.at[0, part], store_sems.at[i, n]))
    for load in loads:
        load.start()
    for load, store in zip(loads, stores):
        load.wait()
        store.start()
    for store in stores:
        store.wait()


def local(tokens, out_grad, gate_weight, up_weight, down_weight, pair_list):
    rows, depth = tokens.shape
    width = gate_weight.shape[1]
    half = rows * DP // 4
    piece = half // CHIPS
    any_space = pl.BlockSpec(memory_space=pl.ANY)
    hbm = pl.BlockSpec(memory_space=pltpu.HBM)
    tile = jax.ShapeDtypeStruct((1, width, width), f32)

    def vmem(shape, kind):
        return pltpu.VMEM(shape, kind)

    scratch = [
        vmem((DP, rows, depth), bf16), vmem((DP, rows, depth), bf16),
        vmem((width, depth), bf16), vmem((width, depth), bf16), vmem((width, depth), bf16),
        vmem((GROUP, 8, 128), i32), pltpu.SMEM((GROUP, 8, 128), i32),
        vmem((2, half, 2 * width), f32), vmem((2, half, 2 * width), f32),
        vmem((1, half, 2 * width), f32), vmem((1, half, 2 * width), f32),
        vmem((2, half, 2 * width), f32), vmem((1, half, 2 * width), f32),
        vmem((CHIPS, 2, piece, 2 * width), i16), vmem((CHIPS - 1, 2, piece, 2 * width), i16),
        vmem((CHIPS, 1, piece, 2 * width), i16), vmem((CHIPS - 1, 1, piece, 2 * width), i16),
        vmem((CHIPS, 2, 8, 128), f32), vmem((CHIPS - 1, 2, 8, 128), f32),
        vmem((CHIPS, 1, 8, 128), f32), vmem((CHIPS - 1, 1, 8, 128), f32),
        vmem((GROUP, piece, 2 * width), bf16), vmem((GROUP, piece, 2 * width), bf16),
        vmem((5 * YH, piece, 2 * width), bf16), vmem((5 * YH, piece, 2 * width), bf16),
        vmem((YH, piece, 2 * width), bf16),
        vmem((GROUP, piece, 2 * width), bf16), vmem((GROUP, piece, 2 * width), bf16),
        vmem((GROUP, piece, 2 * width), bf16), vmem((GROUP, piece, 2 * width), bf16),
        vmem((width, width), f32), vmem((width, width), f32),
        pltpu.SemaphoreType.DMA((5,)), pltpu.SemaphoreType.DMA((256,)), pltpu.SemaphoreType.DMA((256,)),
    ]
    tiles = pl.pallas_call(
        kernel,
        out_shape=(tile, tile),
        in_specs=[hbm] * 5 + [pl.BlockSpec(memory_space=pltpu.SMEM)],
        out_specs=(any_space, any_space),
        scratch_shapes=scratch,
        compiler_params=pltpu.CompilerParams(
            collective_id=0, has_side_effects=True, vmem_limit_bytes=60 * 1024 * 1024),
        name="covariance",
    )(tokens, out_grad, gate_weight.T, up_weight.T, down_weight, pair_list)
    return pl.pallas_call(
        hand_over,
        out_shape=(tile, tile),
        in_specs=[hbm, hbm],
        out_specs=(hbm, hbm),
        scratch_shapes=[vmem((2, 4, width // 4, width), f32), pltpu.SemaphoreType.DMA((2, 4)), pltpu.SemaphoreType.DMA((2, 4))],
        compiler_params=pltpu.CompilerParams(vmem_limit_bytes=60 * 1024 * 1024),
        name="results",
    )(*tiles)


def solution(mesh):
    in_specs = (
        P("dp", "tensor"),
        P("dp", "tensor"),
        P("tensor", "dp"),
        P("tensor", "dp"),
        P("dp", "tensor"),
        P(("dp", "tensor"), None),
    )
    out_specs = (P(("dp", "tensor"), None, None), P(("dp", "tensor"), None, None))
    return jax.shard_map(local, mesh=mesh, in_specs=in_specs, out_specs=out_specs, check_vma=False)
```

```python
import jax
import jax.numpy as jnp
from jax import lax
from jax.experimental import pallas as pl
from jax.experimental.pallas import tpu as pltpu
from jax.sharding import PartitionSpec as P

Z, YH, X, YL, CORES = 8, 4, 4, 2, 2
DP, GROUP = Z * YH, X * YL * CORES
CHIPS = X * YL
LEVELS = 32760.0
MESH = pl.DeviceIdType.MESH
f32, bf16, i16, i32 = jnp.float32, jnp.bfloat16, jnp.int16, jnp.int32


def encode(value, largest):
    root = jnp.sqrt(jnp.abs(value)) * (LEVELS * lax.rsqrt(largest))
    code = (root + 0.5).astype(i32)
    return jnp.where(value < 0, -code, code).astype(i16)


def decode(code, unit):
    root = code.astype(i32).astype(f32)
    return root * jnp.abs(root) * unit


def fold(rows):
    half = rows.shape[0] // 2
    return jnp.concatenate([rows[:half], rows[half:]], axis=1)


def unfold(folded):
    width = folded.shape[1] // 2
    return jnp.concatenate([folded[:, :width], folded[:, width:]], axis=0)


def kernel(tok_in, grd_in, wg_in, wu_in, wd_in, pair, act_out, grad_out,
           x_tok, x_grd, wg, wu, wd, pair_tiles, pair_smem,
           ps_act, pr_act, ps_grd, pr_grd, sum_act, sum_grd,
           cs_act, cr_act, cs_grd, cr_grd, us_act, ur_act, us_grd, ur_grd,
           own_act, own_grd, far_act, far_grd, pass_grd, st_act, st_grd, b_act, b_grd,
           tile_act, tile_grd, local_sem, send_sem, recv_sem):
    dp, tensor = lax.axis_index("dp"), lax.axis_index("tensor")
    z, yh = dp // YH, dp % YH
    core, chip = tensor % CORES, tensor // CORES
    x, yl = chip // YL, chip % YL

    def at(dz=0, dyh=0):
        return ((z + dz + Z) % Z * YH + (yh + dyh + YH) % YH, tensor)

    def in_group(dx, dyl, dc, sign=1):
        return (((x + sign * dx + X) % X * YL + (yl + dyl) % YL) * CORES + (core + dc) % CORES)

    used = [0]
    sent = []

    def send(src, dst, device, only=None):
        n = used[0]
        used[0] += 1
        copy = pltpu.make_async_remote_copy(
            src_ref=src, dst_ref=dst, send_sem=send_sem.at[n], recv_sem=recv_sem.at[n],
            device_id=device, device_id_type=MESH)
        if only is None:
            copy.start()
        else:
            pl.when(only)(copy.start)
        sent.append((only, copy))
        return copy

    peers = [(dx, dyl, dc) for dyl in (1, 0) for dx in (2, 1, 3, 0) for dc in (0, 1) if (dx, dyl, dc) != (0, 0, 0)]
    chip_peers = [(dx, dyl) for dyl in (1, 0) for dx in (2, 1, 3, 0) if (dx, dyl) != (0, 0)]

    barrier = pltpu.get_barrier_semaphore()
    partners = [at(dyh=k) for k in (1, 2, 3)] + [at(dz=k) for k in (1, -1, 2, -2, 3, -3, 4)] + [(dp, in_group(*o)) for o in peers]
    for partner in partners:
        pl.semaphore_signal(barrier, inc=1, device_id=partner, device_id_type=MESH)
    loads = [pltpu.make_async_copy(tok_in, x_tok.at[dp], local_sem.at[0]),
             pltpu.make_async_copy(grd_in, x_grd.at[dp], local_sem.at[1]),
             pltpu.make_async_copy(wg_in, wg, local_sem.at[2]),
             pltpu.make_async_copy(wu_in, wu, local_sem.at[3]),
             pltpu.make_async_copy(wd_in, wd, local_sem.at[4])]
    for load in loads:
        load.start()
    distance = (pair[0, 1] - pair[0, 0] + DP) % DP
    pair_tiles[tensor] = jnp.full((8, 128), distance, i32)
    pl.semaphore_wait(barrier, len(partners))

    def y_slot(k):
        return (yh - k + YH) % YH

    ring = {}

    def along_z(b, buf, src, k):
        slot = z * YH + y_slot(k)
        for step in (2, 1):
            for way in (1, -1):
                ring[b, way, step, k] = send(src, buf.at[slot], at(dz=way * step))

    def pass_along_z(b, buf, k):
        for way in (1, -1):
            ring[b, way, 2, k].wait_recv()
            slot = (z - way * 2 + Z) % Z * YH + y_slot(k)
            if (way == 1) == (k in (0, 2)):
                ring[b, way, 4, k] = send(buf.at[slot], buf.at[slot], at(dz=way * 2))
            ring[b, way, 3, k] = send(buf.at[slot], buf.at[slot], at(dz=way))

    def all_rows(b):
        for k in range(YH):
            for way in (1, -1):
                ring[b, way, 1, k].wait_recv()
                ring[b, way, 3, k].wait_recv()
                if (b, way, 4, k) in ring:
                    ring[b, way, 4, k].wait_recv()

    y_tok = {}
    shifts = (4, 3, -3, 2, -2, 1, -1)
    z_tok = {}

    def to_all_z(src, k):
        slot = z * YH + y_slot(k)
        for shift in shifts:
            z_tok[shift, k] = send(src, x_tok.at[slot], at(dz=shift))

    y_tok[0, 2] = send(tok_in, x_tok.at[dp], at(dyh=2))
    to_all_z(tok_in, 0)
    for k in (1, 3):
        y_tok[0, k] = send(tok_in, x_tok.at[dp], at(dyh=k))
    y_grd = {k: send(grd_in, x_grd.at[dp], at(dyh=k)) for k in (2, 1, 3)}
    along_z(1, x_grd, grd_in, 0)
    pair_copies = [send(pair_tiles.at[tensor], pair_tiles.at[tensor], (dp, in_group(*o))) for o in peers]

    def to_neighbours(shift):
        slot = (z - shift + Z) % Z * YH + yh
        for k in (1, 3):
            y_tok[shift, k] = send(x_tok.at[slot], x_tok.at[slot], at(dyh=k))

    for shift in (1, -1, 2, -2):
        z_tok[shift, 0].wait_recv()
        to_neighbours(shift)
    y_tok[0, 2].wait_recv()
    to_all_z(x_tok.at[z * YH + y_slot(2)], 2)
    for k in (1, 3, 2):
        y_grd[k].wait_recv()
        along_z(1, x_grd, x_grd.at[z * YH + y_slot(k)], k)
    for shift in (3, -3, 4):
        z_tok[shift, 0].wait_recv()
        to_neighbours(shift)
    for load in loads:
        load.wait()

    other = (dp, in_group(0, 0, 1))
    piece = cs_act.shape[2]

    def product(buf, half, weight):
        rows = buf[pl.ds(half * (DP // 2), DP // 2)].reshape(buf.shape[1] * DP // 2, buf.shape[2])
        return fold(lax.dot_general(rows, weight[...], (((1,), (1,)), ((), ())), preferred_element_type=f32))

    def for_other(buf, weights, ps, pr):
        pairs = []
        for i, weight in enumerate(weights):
            ps[i] = product(buf, 1 - core, weight)
            pairs.append(send(ps.at[i], pr.at[i], other))
        return pairs

    def rows_of_chip(q):
        return pl.ds(pl.multiple_of(q * piece, piece), piece)

    def spread(pairs, total, pr, cs, us, cr, ur):
        for pair_copy in pairs:
            pair_copy.wait_recv()
        largest = {}
        for dx, dyl in chip_peers:
            q = in_group(dx, dyl, 0) // CORES
            for i in range(total.shape[0]):
                summed = total[i, rows_of_chip(q)] + pr[i, rows_of_chip(q)]
                total[i, rows_of_chip(q)] = summed
                most = jnp.max(jnp.max(jnp.abs(summed), axis=0, keepdims=True), axis=1, keepdims=True)
                largest[dx, dyl, i] = jnp.maximum(most, 1e-30)
        copies = []
        for n, (dx, dyl) in enumerate(chip_peers):
            there = in_group(dx, dyl, 0)
            q = there // CORES
            for i in range(total.shape[0]):
                most = largest[dx, dyl, i]
                us[q, i] = jnp.broadcast_to(most * (1.0 / (LEVELS * LEVELS)), (8, 128))
                cs[q, i] = encode(total[i, rows_of_chip(q)], most)
            copies.append((send(us.at[q], ur.at[n], (dp, there)), send(cs.at[q], cr.at[n], (dp, there))))
        return copies

    def gathered(copies, total, pr, cr, ur):
        mine = [total[i, rows_of_chip(chip)] + pr[i, rows_of_chip(chip)] for i in range(total.shape[0])]
        for n, copy in enumerate(copies):
            for c in copy:
                c.wait_recv()
            for i in range(total.shape[0]):
                mine[i] += decode(cr[n, i], ur[n, i, 0:1, 0:1])
        return mine

    pass_along_z(1, x_grd, 0)
    for shift in reversed(shifts):
        z_tok[shift, 2].wait_recv()
    for shift in (0, 1, -1, 2, -2, 3, -3, 4):
        for k in (1, 3):
            y_tok[shift, k].wait_recv()
    pairs = for_other(x_tok, (wg, wu), ps_act, pr_act)
    for k in (1, 3, 2):
        pass_along_z(1, x_grd, k)
    for i, weight in enumerate((wg, wu)):
        sum_act[i] = product(x_tok, core, weight)
    c_act = spread(pairs, sum_act, pr_act, cs_act, us_act, cr_act, ur_act)
    all_rows(1)
    pairs = for_other(x_grd, (wd,), ps_grd, pr_grd)
    sum_grd[0] = product(x_grd, core, wd)
    c_grd = spread(pairs, sum_grd, pr_grd, cs_grd, us_grd, cr_grd, ur_grd)

    for copy in pair_copies:
        copy.wait_recv()
    to_smem = pltpu.make_async_copy(pair_tiles, pair_smem, local_sem.at[0])
    to_smem.start()
    to_smem.wait()

    far_x = (2, 1, 3)

    def share_out(own):
        across = send(own.at[tensor], own.at[tensor], (dp, in_group(0, 1, 0)))
        along = [send(own.at[tensor], own.at[tensor], (dp, in_group(dx, 0, 0))) for dx in far_x]
        return across, along, [send(own.at[tensor], own.at[tensor], other)]

    def pass_across(own, across, along, second):
        across.wait_recv()
        slot = in_group(0, 1, 0)
        along += [send(own.at[slot], own.at[slot], (dp, in_group(dx, 0, 0))) for dx in far_x]
        second.append(send(own.at[slot], own.at[slot], other))

    def pass_on(own, across, along, second):
        for n, copy in enumerate(along):
            copy.wait_recv()
            slot = in_group(far_x[n % 3], n // 3, 0, sign=-1)
            second.append(send(own.at[slot], own.at[slot], other))

    def straight_down(far, k, e_z):
        slot = y_slot(k)
        for d in (4, 3, 2, 1):
            e_z[d, k] = send(far.at[slot], far.at[d * YH + slot], at(dz=-d), None if d < 4 or k == 0 else slot <= yh)

    def over_y(far, e_y, hop):
        slot = hop * YH + yh
        for k in (1, 3):
            only = {0: (yh + k) % YH < yh, 4: (yh + k) % YH > yh}.get(hop)
            e_y[hop, k] = send(far.at[slot], far.at[slot], at(dyh=k), only)

    def down_z(far, through, k, e_z):
        slot = y_slot(k)
        e_z[2, k] = send(far.at[slot], far.at[2 * YH + slot], at(dz=-2))
        e_z[-2, k] = send(far.at[slot], through.at[slot], at(dz=2), None if k == 0 else slot <= yh)
        e_z[1, k] = send(far.at[slot], far.at[YH + slot], at(dz=-1))

    def pass_down_z(far, through, k, e_z):
        slot = y_slot(k)
        e_z[2, k].wait_recv()
        e_z[3, k] = send(far.at[2 * YH + slot], far.at[3 * YH + slot], at(dz=-1))
        if k == 0:
            e_z[-2, k].wait_recv()
            e_z[4, k] = send(through.at[slot], far.at[4 * YH + slot], at(dz=2))
        else:
            pl.when(slot <= yh)(e_z[-2, k].wait_recv)
            e_z[4, k] = send(through.at[slot], far.at[4 * YH + slot], at(dz=2), slot <= yh)

    gate, up = gathered(c_act, sum_act, pr_act, cr_act, ur_act)
    hidden = (gate / (1.0 + jnp.exp(-gate)) * up).astype(bf16)
    own_act[tensor] = hidden
    far_act[yh] = hidden
    act_z, act_y = {}, {}
    act_opposite = send(far_act.at[yh], far_act.at[yh], at(dyh=2))
    straight_down(far_act, 0, act_z)
    over_y(far_act, act_y, 0)
    d_act = share_out(own_act)

    (grad_sum,) = gathered(c_grd, sum_grd, pr_grd, cr_grd, ur_grd)
    hidden_grad = grad_sum.astype(bf16)
    own_grd[tensor] = hidden_grad
    far_grd[yh] = hidden_grad
    grd_z, grd_y = {}, {}
    grd_opposite = send(far_grd.at[yh], far_grd.at[yh], at(dyh=2))
    down_z(far_grd, pass_grd, 0, grd_z)
    over_y(far_grd, grd_y, 0)
    d_grd = share_out(own_grd)

    for hop in (1, 2):
        act_z[hop, 0].wait_recv()
        over_y(far_act, act_y, hop)
    act_opposite.wait_recv()
    straight_down(far_act, 2, act_z)
    for hop in (3, 4):
        act_z[hop, 0].wait_recv()
        over_y(far_act, act_y, hop)
    grd_z[1, 0].wait_recv()
    over_y(far_grd, grd_y, 1)
    pass_down_z(far_grd, pass_grd, 0, grd_z)
    over_y(far_grd, grd_y, 2)
    grd_opposite.wait_recv()
    down_z(far_grd, pass_grd, 2, grd_z)
    pass_across(own_act, *d_act)
    pass_across(own_grd, *d_grd)
    for hop in (3, 4):
        grd_z[hop, 0].wait_recv()
        over_y(far_grd, grd_y, hop)
    pass_down_z(far_grd, pass_grd, 2, grd_z)
    pass_on(own_act, *d_act)

    def deliver(far, st, b):
        for j in range(GROUP):
            st[j] = far[yh + pair_smem[j, 0, 0]]
        copies = [send(st.at[in_group(*o)], b.at[tensor], (dp, in_group(*o))) for o in peers]
        b[tensor] = st[tensor]
        return copies

    def all_far(e_z, e_y, steps):
        for step in steps:
            e_z[step, 2].wait_recv()
        pl.when(y_slot(2) <= yh)(e_z[4, 2].wait_recv)
        for k in (1, 3):
            there = y_slot(k)
            pl.when(yh < there)(e_y[0, k].wait_recv)
            for hop in (1, 2, 3):
                e_y[hop, k].wait_recv()
            pl.when(yh > there)(e_y[4, k].wait_recv)

    all_far(act_z, act_y, (1, 2, 3))
    before = len(sent)
    e_act = deliver(far_act, st_act, b_act)
    pass_on(own_grd, *d_grd)
    all_far(grd_z, grd_y, (1, 3))
    e_grd = deliver(far_grd, st_grd, b_grd)

    diagonal = (distance == DP // 2) & (dp >= DP // 2)
    is_diagonal = jnp.full((1, 1), jnp.where(diagonal, 1, 0), i32) == 1

    def tile(own, b, second, delivered, out):
        for copy in second + delivered:
            copy.wait_recv()
        left = unfold(own[...].reshape(GROUP * piece, own.shape[2]))
        far = unfold(b[...].reshape(GROUP * piece, b.shape[2]))
        right = jnp.where(jnp.broadcast_to(is_diagonal, far.shape), left, far)
        dims = (((0,), (0,)), ((), ()))
        upper = lax.dot_general(left, right, dims, preferred_element_type=f32)
        lower = lax.dot_general(far, far, dims, preferred_element_type=f32)
        p = lax.broadcasted_iota(i32, upper.shape, 0)
        q = lax.broadcasted_iota(i32, upper.shape, 1)
        take_lower = jnp.where(p > q, jnp.where(is_diagonal, 1, 0), 0) == 1
        out[...] = jnp.where(take_lower, lower, upper) * (1.0 / (DP * 16))

    def finish(copies):
        for only, copy in copies:
            if only is None:
                copy.wait_send()
            else:
                pl.when(only)(copy.wait_send)

    finish(sent[:before])
    tile(own_act, b_act, d_act[2], e_act, tile_act)
    write_act = pltpu.make_async_copy(tile_act, act_out.at[0], local_sem.at[1])
    write_act.start()
    tile(own_grd, b_grd, d_grd[2], e_grd, tile_grd)
    write_grd = pltpu.make_async_copy(tile_grd, grad_out.at[0], local_sem.at[2])
    write_grd.start()

    finish(sent[before:])
    write_act.wait()
    write_grd.wait()


def hand_over(act, grad, act_out, grad_out, held, load_sems, store_sems):
    parts, rows = held.shape[1], held.shape[2]
    loads, stores = [], []
    for i, (source, target) in enumerate(((act, act_out), (grad, grad_out))):
        for n in range(parts):
            part = pl.ds(n * rows, rows)
            loads.append(pltpu.make_async_copy(source.at[0, part], held.at[i, n], load_sems.at[i, n]))
            stores.append(pltpu.make_async_copy(held.at[i, n], target.at[0, part], store_sems.at[i, n]))
    for load in loads:
        load.start()
    for load, store in zip(loads, stores):
        load.wait()
        store.start()
    for store in stores:
        store.wait()


def local(tokens, out_grad, gate_weight, up_weight, down_weight, pair_list):
    rows, depth = tokens.shape
    width = gate_weight.shape[1]
    half = rows * DP // 4
    piece = half // CHIPS
    any_space = pl.BlockSpec(memory_space=pl.ANY)
    hbm = pl.BlockSpec(memory_space=pltpu.HBM)
    tile = jax.ShapeDtypeStruct((1, width, width), f32)

    def vmem(shape, kind):
        return pltpu.VMEM(shape, kind)

    scratch = [
        vmem((DP, rows, depth), bf16), vmem((DP, rows, depth), bf16),
        vmem((width, depth), bf16), vmem((width, depth), bf16), vmem((width, depth), bf16),
        vmem((GROUP, 8, 128), i32), pltpu.SMEM((GROUP, 8, 128), i32),
        vmem((2, half, 2 * width), f32), vmem((2, half, 2 * width), f32),
        vmem((1, half, 2 * width), f32), vmem((1, half, 2 * width), f32),
        vmem((2, half, 2 * width), f32), vmem((1, half, 2 * width), f32),
        vmem((CHIPS, 2, piece, 2 * width), i16), vmem((CHIPS - 1, 2, piece, 2 * width), i16),
        vmem((CHIPS, 1, piece, 2 * width), i16), vmem((CHIPS - 1, 1, piece, 2 * width), i16),
        vmem((CHIPS, 2, 8, 128), f32), vmem((CHIPS - 1, 2, 8, 128), f32),
        vmem((CHIPS, 1, 8, 128), f32), vmem((CHIPS - 1, 1, 8, 128), f32),
        vmem((GROUP, piece, 2 * width), bf16), vmem((GROUP, piece, 2 * width), bf16),
        vmem((5 * YH, piece, 2 * width), bf16), vmem((5 * YH, piece, 2 * width), bf16),
        vmem((YH, piece, 2 * width), bf16),
        vmem((GROUP, piece, 2 * width), bf16), vmem((GROUP, piece, 2 * width), bf16),
        vmem((GROUP, piece, 2 * width), bf16), vmem((GROUP, piece, 2 * width), bf16),
        vmem((width, width), f32), vmem((width, width), f32),
        pltpu.SemaphoreType.DMA((5,)), pltpu.SemaphoreType.DMA((256,)), pltpu.SemaphoreType.DMA((256,)),
    ]
    tiles = pl.pallas_call(
        kernel,
        out_shape=(tile, tile),
        in_specs=[hbm] * 5 + [pl.BlockSpec(memory_space=pltpu.SMEM)],
        out_specs=(any_space, any_space),
        scratch_shapes=scratch,
        compiler_params=pltpu.CompilerParams(
            collective_id=0, has_side_effects=True, vmem_limit_bytes=60 * 1024 * 1024),
        name="covariance",
    )(tokens, out_grad, gate_weight.T, up_weight.T, down_weight, pair_list)
    return pl.pallas_call(
        hand_over,
        out_shape=(tile, tile),
        in_specs=[hbm, hbm],
        out_specs=(hbm, hbm),
        scratch_shapes=[vmem((2, 4, width // 4, width), f32), pltpu.SemaphoreType.DMA((2, 4)), pltpu.SemaphoreType.DMA((2, 4))],
        compiler_params=pltpu.CompilerParams(vmem_limit_bytes=60 * 1024 * 1024),
        name="results",
    )(*tiles)


def solution(mesh):
    in_specs = (
        P("dp", "tensor"),
        P("dp", "tensor"),
        P("tensor", "dp"),
        P("tensor", "dp"),
        P("dp", "tensor"),
        P(("dp", "tensor"), None),
    )
    out_specs = (P(("dp", "tensor"), None, None), P(("dp", "tensor"), None, None))
    return jax.shard_map(local, mesh=mesh, in_specs=in_specs, out_specs=out_specs, check_vma=False)
```
